32 devices in a mesh: grp: 2 (over y), ta: 4 (over z), ha: 4 (over x, core).
Axes of the slice: x: 2, y: 2, z: 4, core: 2. Of those that a mesh axis runs over, the one named last changes fastest.
Arguments:
- queries: bfloat16 [48, 16, 8, 1536], P(('grp', 'ta'), 'ha'), parts along dimension 0, may hold values from -6 to 6
- key_rows: bfloat16 [48, 16, 8, 1536], P(('grp', 'ta'), 'ha'), parts along dimension 0, may hold values from -6 to 6
- value_rows: bfloat16 [48, 16, 8, 1536], P(('grp', 'ta'), 'ha'), parts along dimension 0, may hold values from -6 to 6
- out_grad: bfloat16 [48, 16, 8, 1536], P(('grp', 'ta'), 'ha'), parts along dimension 0, may hold values from -192 to 192
- logsumexp: float32 [48, 16, 8, 12], P(('grp', 'ta'), 'ha'), parts along dimension 0, may hold values from 6.5 to 8.5
- out_dot: float32 [48, 16, 8, 12], P(('grp', 'ta'), 'ha'), parts along dimension 0, may hold values from -384 to 384
- text_keys: bfloat16 [256, 1536], P(('grp', 'ta')), parts along dimension 0, may hold values from -6 to 6
- text_values: bfloat16 [256, 1536], P(('grp', 'ta')), parts along dimension 0, may hold values from -6 to 6
- text_length: int32 [2], P('grp'), parts along dimension 0, may hold values from 16 to 128
- window_reach: int32 [12, 2], replicated, may hold values from 0 to 1
Outputs:
- query_grad: bfloat16 [48, 16, 8, 1536], P(('grp', 'ta'), 'ha'), parts along dimension 0
- key_grad: bfloat16 [48, 16, 8, 1536], P(('grp', 'ta'), 'ha'), parts along dimension 0
- value_grad: bfloat16 [48, 16, 8, 1536], P(('grp', 'ta'), 'ha'), parts along dimension 0
- text_key_grad: bfloat16 [256, 1536], P(('grp', 'ta')), parts along dimension 0
- text_value_grad: bfloat16 [256, 1536], P(('grp', 'ta')), parts along dimension 0
The draws below stay inside these ranges and needn't reach their ends.
There are 2 independent parts, one for each index of `grp`. The reference program is written for one: setup_inputs(seed, part) draws one part's arguments, and reference() takes and returns one part's arrays. A program takes and returns all parts, laid end to end along the dimension named above; an argument that names none is the same for every part. Nothing has to cross between parts.
All inputs are finite; a program needn't handle non-finite values.
Results may differ from the reference program's by a relative error of at most 0.0059.
Values may be sent and summed in bfloat16 or wider, within the bound.
A program may use at most 128 MiB of HBM per device.

```python
import jax
import jax.numpy as jnp
from jax import lax

TILE_T = 6
TILE_H = 8
HEADS = 12
HEAD_DIM = 128
TEXT = 128
WT = 1
WIDTH = 8
HD = 1536
FRAMES = 24
HEIGHT = 16
N_TA = 4
N_HA = 4


def touch_ends(values, own_key, smallest, top_value):
    longest = values.shape.index(max(values.shape))
    spots = []
    for shift in (0, 1):
        where = [jax.random.randint(jax.random.fold_in(own_key, axis), (), 0, length) for axis, length in enumerate(values.shape)]
        where[longest] = (where[longest] + shift) % values.shape[longest]
        spots.append(tuple(where))
    return values.at[spots[0]].set(smallest).at[spots[1]].set(top_value)


def shard_levels(own_key, extent, pieces, smallest, top_value):
    level, own = 1.0, jax.random.fold_in(own_key, 6)
    for dim, shards_of in pieces:
        heights = jnp.exp(jax.random.uniform(jax.random.fold_in(own, dim), (shards_of,), jnp.float32, smallest / len(pieces), top_value / len(pieces)))
        level = level * jnp.repeat(heights, extent[dim] // shards_of).reshape([-1 if axis == dim else 1 for axis in range(len(extent))])
    return level


def scatter_about(own_key, shape, spread, most, split=(), kind=jnp.bfloat16):
    result = spread * jax.random.normal(own_key, shape, jnp.float32)
    if split:
        result = result * shard_levels(own_key, shape, split, -0.22, 0.18)
    return jnp.clip(result, -most, most).astype(kind)


def setup_inputs(seed: int = 0, part: int = 0) -> dict:
    seeds = jax.random.split(jax.random.key(seed), 11)
    part_keys = jax.random.split(jax.random.fold_in(seeds[10], part), 11)
    queries = scatter_about(part_keys[0], (FRAMES, HEIGHT, WIDTH, HD), 1.0, 6.0, ((0, 4), (1, 4)))
    key_rows = scatter_about(part_keys[1], (FRAMES, HEIGHT, WIDTH, HD), 1.0, 6.0, ((0, 4), (1, 4)))
    value_rows = scatter_about(part_keys[2], (FRAMES, HEIGHT, WIDTH, HD), 1.0, 6.0, ((0, 4), (1, 4)))
    out_grad = scatter_about(part_keys[3], (FRAMES, HEIGHT, WIDTH, HD), 30.0, 192.0, ((0, 4), (1, 4)))
    logsumexp = jnp.clip(6.5 + 2.0 * jax.random.uniform(part_keys[4], (FRAMES, HEIGHT, WIDTH, HEADS), jnp.float32) ** shard_levels(part_keys[4], (FRAMES, HEIGHT, WIDTH, HEADS), ((0, 4), (1, 4)), -0.2, 0.2), 6.5, 8.5)
    out_dot = scatter_about(part_keys[5], (FRAMES, HEIGHT, WIDTH, HEADS), 60.0, 384.0, ((0, 4), (1, 4)), jnp.float32)
    text_keys = scatter_about(part_keys[6], (TEXT, HD), 1.0, 6.0, ((0, 4),))
    text_values = scatter_about(part_keys[7], (TEXT, HD), 1.0, 6.0, ((0, 4),))
    text_length = jax.random.randint(part_keys[8], (1,), 16, TEXT + 1).astype(jnp.int32)
    window_reach = touch_ends(jax.random.randint(seeds[9], (HEADS, 2), 0, 2), jax.random.fold_in(seeds[9], 1), 0, 1).astype(jnp.int32)
    return {"queries": queries, "key_rows": key_rows, "value_rows": value_rows, "out_grad": out_grad, "logsumexp": logsumexp, "out_dot": out_dot, "text_keys": text_keys, "text_values": text_values, "text_length": text_length, "window_reach": window_reach}


def as_data(values):
    return lax.optimization_barrier(values.astype(jnp.bfloat16)).astype(jnp.float32)


def widen(values):
    return values.astype(jnp.float32)


def pair_grads(query_set, grad_set, logsum_set, dot_set, key_set, value_set, allowed, scaling, band_rows, width_tiles):
    query_tiles = query_set.shape[0]
    frames = query_set.shape[1]
    query_band = query_set.shape[2]
    width_cols = query_set.shape[3]
    head_size = query_set.shape[4]
    key_tiles = key_set.shape[0]
    key_band = key_set.shape[2]
    tile_cols = width_cols // width_tiles
    query_shape = (query_tiles, frames, query_band // band_rows, band_rows, width_tiles, tile_cols, head_size)
    key_shape = (key_tiles, frames, key_band // band_rows, band_rows, width_tiles, tile_cols, head_size)
    stat_shape = (query_tiles, frames, query_band // band_rows, band_rows, width_tiles, tile_cols)
    query_grid = widen(query_set).reshape(query_shape)
    grad_grid = widen(grad_set).reshape(query_shape)
    key_grid = widen(key_set).reshape(key_shape)
    value_grid = widen(value_set).reshape(key_shape)
    logsum_grid = logsum_set.reshape(stat_shape).transpose(4, 0, 1, 2, 3, 5)[..., None, None, None, None, None]
    dot_grid = dot_set.reshape(stat_shape).transpose(4, 0, 1, 2, 3, 5)[..., None, None, None, None, None]
    pattern = "atgywxd,buhzwvd->watgyxbuhzv"
    scores = jnp.einsum(pattern, query_grid, key_grid)
    visible = allowed[None, :, None, None, None, None, :, None, None, None, None]
    weight = jnp.where(visible, jnp.exp(scores * scaling - logsum_grid), 0.0)
    prob_data = as_data(weight)
    prob_grad = jnp.einsum(pattern, grad_grid, value_grid)
    score_grad = as_data(weight * (prob_grad - dot_grid) * scaling)
    query_terms = jnp.einsum("watgyxbuhzv,buhzwvd->atgywxbhd", score_grad, key_grid)
    key_terms = jnp.einsum("watgyxbuhzv,atgywxd->buhzwvagd", score_grad, query_grid)
    value_terms = jnp.einsum("watgyxbuhzv,atgywxd->buhzwvagd", prob_data, grad_grid)
    query_part = jnp.sum(as_data(query_terms), axis=(6, 7)).reshape(query_tiles, frames, query_band, width_cols, head_size)
    key_part = jnp.sum(as_data(key_terms), axis=(6, 7)).reshape(key_tiles, frames, key_band, width_cols, head_size)
    value_part = jnp.sum(as_data(value_terms), axis=(6, 7)).reshape(key_tiles, frames, key_band, width_cols, head_size)
    return query_part, key_part, value_part


def text_grads(query_part, grad_part, logsum_part, dot_part, text_key_part, text_value_part, text_ok, scaling, width_tiles):
    frames = query_part.shape[0]
    band_rows = query_part.shape[1]
    width_cols = query_part.shape[2]
    head_size = query_part.shape[3]
    tile_cols = width_cols // width_tiles
    query_grid = widen(query_part).reshape(frames, band_rows, width_tiles, tile_cols, head_size)
    grad_grid = widen(grad_part).reshape(frames, band_rows, width_tiles, tile_cols, head_size)
    logsum_grid = logsum_part.reshape(frames, band_rows, width_tiles, tile_cols).transpose(2, 0, 1, 3)[..., None]
    dot_grid = dot_part.reshape(frames, band_rows, width_tiles, tile_cols).transpose(2, 0, 1, 3)[..., None]
    text_key_data = widen(text_key_part)
    text_value_data = widen(text_value_part)
    scores = jnp.einsum("tywxd,jd->wtyxj", query_grid, text_key_data)
    weight = jnp.where(text_ok, jnp.exp(scores * scaling - logsum_grid), 0.0)
    prob_data = as_data(weight)
    prob_grad = jnp.einsum("tywxd,jd->wtyxj", grad_grid, text_value_data)
    score_grad = as_data(weight * (prob_grad - dot_grid) * scaling)
    text_query = jnp.einsum("wtyxj,jd->tywxd", score_grad, text_key_data).reshape(frames, band_rows, width_cols, head_size)
    text_key = jnp.einsum("wtyxj,tywxd->jd", score_grad, query_grid)
    text_value = jnp.einsum("wtyxj,tywxd->jd", prob_data, grad_grid)
    return text_query, text_key, text_value


def reference(queries, key_rows, value_rows, out_grad, logsumexp, out_dot, text_keys, text_values, text_length, window_reach):
    band_rows = TILE_H // 2
    scaling = HEAD_DIM ** -0.5
    padding = ((TILE_T, TILE_T), (0, 0), (0, 0), (0, 0))
    key_padded = jnp.pad(key_rows, padding)
    value_padded = jnp.pad(value_rows, padding)
    text_ok = jnp.arange(TEXT, dtype=jnp.int32) < text_length[0]
    offsets = jnp.arange(3, dtype=jnp.int32) - 1
    own_shape = (TILE_T, band_rows, WIDTH, HD)
    stat_shape = (TILE_T, band_rows, WIDTH, HEADS)
    ext_shape = (3 * TILE_T, TILE_H, WIDTH, HD)
    grid_shape = (3, TILE_T, TILE_H, WIDTH, HD)

    def block_step(carried, block_index):
        key_total, value_total, key_text_total, value_text_total = carried
        block_index = block_index.astype(jnp.int32)
        time_tile = (block_index // N_HA).astype(jnp.int32)
        band_index = (block_index % N_HA).astype(jnp.int32)
        zero = jnp.zeros((), jnp.int32)
        anchor = ((time_tile * TILE_T).astype(jnp.int32), (band_index * band_rows).astype(jnp.int32), zero, zero)
        ext_anchor = ((time_tile * TILE_T).astype(jnp.int32), ((band_index // 2) * TILE_H).astype(jnp.int32), zero, zero)
        query_block = lax.dynamic_slice(queries, anchor, own_shape)
        grad_block = lax.dynamic_slice(out_grad, anchor, own_shape)
        logsum_block = lax.dynamic_slice(logsumexp, anchor, stat_shape)
        dot_block = lax.dynamic_slice(out_dot, anchor, stat_shape)
        key_ext = lax.dynamic_slice(key_padded, ext_anchor, ext_shape).reshape(grid_shape)
        value_ext = lax.dynamic_slice(value_padded, ext_anchor, ext_shape).reshape(grid_shape)
        tile_ok = jnp.stack([time_tile > 0, time_tile >= 0, time_tile < N_TA - 1])

        def head_step(head_index, head_state):
            query_out, key_out, value_out, key_text, value_text = head_state
            column_start = (head_index * HEAD_DIM).astype(jnp.int32)
            query_part = lax.dynamic_slice_in_dim(query_block, column_start, HEAD_DIM, 3)
            grad_part = lax.dynamic_slice_in_dim(grad_block, column_start, HEAD_DIM, 3)
            logsum_part = lax.dynamic_index_in_dim(logsum_block, head_index, 3, False)
            dot_part = lax.dynamic_index_in_dim(dot_block, head_index, 3, False)
            allowed = (tile_ok & (offsets >= -window_reach[head_index, 0]) & (offsets <= window_reach[head_index, 1]))[None, :]
            query_terms, key_terms, value_terms = pair_grads(
                query_part[None], grad_part[None], logsum_part[None], dot_part[None],
                lax.dynamic_slice_in_dim(key_ext, column_start, HEAD_DIM, 4),
                lax.dynamic_slice_in_dim(value_ext, column_start, HEAD_DIM, 4),
                allowed, scaling, band_rows, WT)
            text_query, text_key, text_value = text_grads(
                query_part, grad_part, logsum_part, dot_part,
                lax.dynamic_slice_in_dim(text_keys, column_start, HEAD_DIM, 1),
                lax.dynamic_slice_in_dim(text_values, column_start, HEAD_DIM, 1),
                text_ok, scaling, WT)
            query_out = lax.dynamic_update_slice_in_dim(query_out, (query_terms[0] + text_query).astype(jnp.bfloat16), column_start, 3)
            key_out = lax.dynamic_update_slice_in_dim(key_out, key_terms, column_start, 4)
            value_out = lax.dynamic_update_slice_in_dim(value_out, value_terms, column_start, 4)
            key_text = lax.dynamic_update_slice_in_dim(key_text, text_key, column_start, 1)
            value_text = lax.dynamic_update_slice_in_dim(value_text, text_value, column_start, 1)
            return query_out, key_out, value_out, key_text, value_text

        initial = (jnp.zeros(own_shape, jnp.bfloat16), jnp.zeros(grid_shape, jnp.float32),
                   jnp.zeros(grid_shape, jnp.float32), jnp.zeros((TEXT, HD), jnp.float32),
                   jnp.zeros((TEXT, HD), jnp.float32))
        query_out, key_out, value_out, key_text, value_text = lax.fori_loop(0, HEADS, head_step, initial)
        key_total = lax.dynamic_update_slice(key_total, lax.dynamic_slice(key_total, ext_anchor, ext_shape) + key_out.reshape(ext_shape), ext_anchor)
        value_total = lax.dynamic_update_slice(value_total, lax.dynamic_slice(value_total, ext_anchor, ext_shape) + value_out.reshape(ext_shape), ext_anchor)
        return (key_total, value_total, key_text_total + key_text, value_text_total + value_text), query_out

    big_zero = jnp.zeros((FRAMES + 2 * TILE_T, HEIGHT, WIDTH, HD), jnp.float32)
    text_zero = jnp.zeros((TEXT, HD), jnp.float32)
    totals, query_blocks = lax.scan(block_step, (big_zero, big_zero, text_zero, text_zero), jnp.arange(N_TA * N_HA, dtype=jnp.int32))
    query_grad = query_blocks.reshape(N_TA, N_HA, TILE_T, band_rows, WIDTH, HD).transpose(0, 2, 1, 3, 4, 5).reshape(FRAMES, HEIGHT, WIDTH, HD)
    key_grad = totals[0][TILE_T:TILE_T + FRAMES].astype(jnp.bfloat16)
    value_grad = totals[1][TILE_T:TILE_T + FRAMES].astype(jnp.bfloat16)
    return (query_grad, key_grad, value_grad, totals[2].astype(jnp.bfloat16), totals[3].astype(jnp.bfloat16))
```

```python
import functools

import jax
import jax.numpy as jnp
from jax import lax
from jax.experimental import pallas as pl
from jax.experimental.pallas import tpu as pltpu
from jax.sharding import PartitionSpec as P

LOG2E = 1.4426950408889634
HIDDEN_LSE = 1e30
MESH_ID = pl.DeviceIdType.MESH
NT = (((1,), (1,)), ((), ()))
NN = (((1,), (0,)), ((), ()))
TN = (((0,), (0,)), ((), ()))


def dot(a, b, dims):
    return lax.dot_general(a, b, dims, preferred_element_type=jnp.float32)


def kernel(
    tiles,
    heads,
    size,
    q_in,
    g_in,
    k_in,
    v_in,
    stat_in,
    text_k,
    text_v,
    length,
    reach,
    q_out,
    k_out,
    v_out,
    tk_out,
    tv_out,
    qw,
    gw,
    kw,
    vw,
    sw,
    st,
    ak,
    av,
    dq,
    dk,
    rq,
    rk,
    local_sem,
    pair_send,
    pair_recv,
    stat_send,
    stat_recv,
    far_send,
    far_recv,
    term_send,
    term_recv,
    kv_send,
    kv_recv,
):
    rows = q_in.shape[0]
    cols = heads * size
    scaling = size ** (-0.5)
    grp = lax.axis_index("grp")
    t = lax.axis_index("ta")
    ha = lax.axis_index("ha")
    c = lax.rem(ha, 2)
    o = 1 - c
    base = ha - c
    partner = (grp, t, base + o)
    has = (t > 0, t < tiles - 1)
    near = (t - 1, t + 1)

    def group(index):
        return pl.ds(pl.multiple_of(index * cols, 128), cols)

    def head(j):
        return pl.ds(pl.multiple_of(j * size, 128), size)

    def group_head(index, j):
        return pl.ds(pl.multiple_of(index * cols + j * size, 128), size)

    barrier = pltpu.get_barrier_semaphore()
    pl.semaphore_signal(barrier, inc=1, device_id=partner, device_id_type=MESH_ID)
    for d in range(2):

        @pl.when(has[d])
        def _():
            for cc in range(2):
                pl.semaphore_signal(
                    barrier, inc=1, device_id=(grp, near[d], base + cc), device_id_type=MESH_ID
                )

    count = 1 + 2 * jnp.where(t > 0, 1, 0) + 2 * jnp.where(t < tiles - 1, 1, 0)
    pl.semaphore_wait(barrier, count)

    def far(d, cc, a, j):
        src = (q_in, g_in)[a]
        dst = (qw, gw)[a]
        return pltpu.make_async_remote_copy(
            src_ref=src.at[:, group_head(cc, j)],
            dst_ref=dst.at[2 - d, c, :, head(j)],
            send_sem=far_send.at[d, cc, a, j],
            recv_sem=far_recv.at[1 - d, c, a, j],
            device_id=(grp, near[d], base + cc),
            device_id_type=MESH_ID,
        )

    def far_wait(d, b, a, j):
        dst = (qw, gw)[a].at[1 + d, b, :, head(j)]
        pltpu.make_async_copy(dst, dst, far_recv.at[d, b, a, j]).wait()

    def stat_far(d, cc):
        return pltpu.make_async_remote_copy(
            src_ref=stat_in.at[cc],
            dst_ref=sw.at[2 - d, c],
            send_sem=stat_send.at[1 + d, cc],
            recv_sem=stat_recv.at[2 - d, c],
            device_id=(grp, near[d], base + cc),
            device_id_type=MESH_ID,
        )

    def pair(a):
        src = (q_in, g_in, k_in, v_in)[a]
        dst = (qw.at[0, c], gw.at[0, c], kw.at[c], vw.at[c])[a]
        return pltpu.make_async_remote_copy(
            src_ref=src.at[:, group(o)],
            dst_ref=dst,
            send_sem=pair_send.at[a],
            recv_sem=pair_recv.at[a],
            device_id=partner,
            device_id_type=MESH_ID,
        )

    def own(a):
        src = (q_in, g_in, k_in, v_in)[a]
        dst = (qw.at[0, c], gw.at[0, c], kw.at[c], vw.at[c])[a]
        return pltpu.make_async_copy(src.at[:, group(c)], dst, local_sem.at[a])

    stat_pair = pltpu.make_async_remote_copy(
        src_ref=stat_in.at[o],
        dst_ref=sw.at[0, c],
        send_sem=stat_send.at[0, 0],
        recv_sem=stat_recv.at[0, 0],
        device_id=partner,
        device_id_type=MESH_ID,
    )

    stat_pair.start()
    for a in range(4):
        pair(a).start()
        own(a).start()
    for d in range(2):

        @pl.when(has[d])
        def _():
            for cc in range(2):
                stat_far(d, cc).start()

    def send_far(j, carry):
        for d in range(2):

            @pl.when(has[d])
            def _():
                for a in range(2):
                    for cc in range(2):
                        far(d, cc, a, j).start()

        return carry

    lax.fori_loop(0, heads, send_far, 0)

    for d in range(2):

        @pl.when(jnp.logical_not(has[d]))
        def _():
            rq[1 + d] = jnp.zeros_like(rq[1 + d])

    for a in range(4):
        own(a).wait()
        pair(a).wait_recv()
    stat_pair.wait_recv()
    st[0] = stat_in[c] + sw[0, o]

    def term(s, b, j):
        target = partner if s == 0 else (grp, near[s - 1], base + b)
        slot = (0, 2, 1)[s]
        return pltpu.make_async_remote_copy(
            src_ref=dq.at[s, b, :, head(j)],
            dst_ref=rq.at[slot, c, :, head(j)],
            send_sem=term_send.at[s, 0 if s == 0 else b, j],
            recv_sem=term_recv.at[slot, c, j],
            device_id=target,
            device_id_type=MESH_ID,
        )

    def term_wait(slot, group_index, j):
        dst = rq.at[slot, group_index, :, head(j)]
        pltpu.make_async_copy(dst, dst, term_recv.at[slot, group_index, j]).wait()

    def kv(a, j):
        return pltpu.make_async_remote_copy(
            src_ref=dk.at[a, o, :, head(j)],
            dst_ref=rk.at[a, :, head(j)],
            send_sem=kv_send.at[a, j],
            recv_sem=kv_recv.at[a, j],
            device_id=partner,
            device_id_type=MESH_ID,
        )

    def both(ref, j):
        return ref[:, :, head(j)].reshape(2 * rows, size)

    def grads(q, g, k, v, lse, out_dot, ok):
        weight = jnp.exp2(dot(k, q, NT) * (scaling * LOG2E) - lse)
        if ok is not None:
            weight = jnp.where(ok, weight, 0.0)
        score = (weight * (dot(v, g, NT) - out_dot) * scaling).astype(jnp.bfloat16)
        prob = weight.astype(jnp.bfloat16)
        return dot(score, k, TN), dot(score, q, NN), dot(prob, g, NN)

    text_ok = lax.broadcasted_iota(jnp.int32, (text_k.shape[0], 1), 0) < length[0]

    def near_step(j, carry):
        q, g = both(qw.at[0], j), both(gw.at[0], j)
        lse, out_dot = st[0, pl.ds(j, 1), :], st[0, pl.ds(8 + j, 1), :]
        dq_own, dk_own, dv_own = grads(q, g, both(kw, j), both(vw, j), lse, out_dot, None)
        tk, tv = text_k[:, group_head(c, j)], text_v[:, group_head(c, j)]
        dq_text, dk_text, dv_text = grads(q, g, tk, tv, lse, out_dot, text_ok)
        ak[:, head(j)] = dk_own
        av[:, head(j)] = dv_own
        tk_out[:, head(j)] = dk_text
        tv_out[:, head(j)] = dv_text
        total = (dq_own + dq_text).astype(jnp.bfloat16)
        dq[0, :, :, head(j)] = total.reshape(2, rows, size)
        term(0, o, j).start()
        return carry

    lax.fori_loop(0, heads, near_step, 0)

    for d in range(2):

        @pl.when(has[d])
        def _():
            for b in range(2):
                dst = sw.at[1 + d, b]
                pltpu.make_async_copy(dst, dst, stat_recv.at[1 + d, b]).wait()
            st[1 + d] = sw[1 + d, 0] + sw[1 + d, 1]

    def far_step(j, carry):
        for d in range(2):

            @pl.when(has[d])
            def _():
                for a in range(2):
                    for b in range(2):
                        far_wait(d, b, a, j)
                seen = reach[c * heads + j, 1 - d] >= 1
                lse = st[1 + d, pl.ds(j, 1), :] + jnp.where(seen, 0.0, HIDDEN_LSE)
                out_dot = st[1 + d, pl.ds(8 + j, 1), :]
                dq_far, dk_far, dv_far = grads(
                    both(qw.at[1 + d], j),
                    both(gw.at[1 + d], j),
                    both(kw, j),
                    both(vw, j),
                    lse,
                    out_dot,
                    None,
                )
                ak[:, head(j)] += dk_far
                av[:, head(j)] += dv_far
                dq[1 + d, :, :, head(j)] = (
                    dq_far.astype(jnp.bfloat16).reshape(2, rows, size)
                )
                for b in range(2):
                    term(1 + d, b, j).start()

        dk[0, :, :, head(j)] = (
            ak[:, head(j)].astype(jnp.bfloat16).reshape(2, rows, size)
        )
        dk[1, :, :, head(j)] = av[:, head(j)].astype(jnp.bfloat16).reshape(2, rows, size)
        for a in range(2):
            kv(a, j).start()
        return carry

    lax.fori_loop(0, heads, far_step, 0)

    k_out[:, group(c)] = dk[0, c]
    v_out[:, group(c)] = dk[1, c]

    def finish(j, carry):
        for a in range(2):
            kv(a, j).wait()
        term(0, o, j).wait_send()
        term_wait(0, o, j)
        for d in range(2):

            @pl.when(has[d])
            def _():
                for b in range(2):
                    term_wait(1 + d, b, j)
                    term(1 + d, b, j).wait_send()
                    for a in range(2):
                        far(d, b, a, j).wait_send()

        return carry

    lax.fori_loop(0, heads, finish, 0)
    stat_pair.wait_send()
    for a in range(4):
        pair(a).wait_send()
    for d in range(2):

        @pl.when(has[d])
        def _():
            for cc in range(2):
                stat_far(d, cc).wait_send()

    k_out[:, group(o)] = rk[0]
    v_out[:, group(o)] = rk[1]

    def total(own_part, index):
        return (
            own_part.astype(jnp.float32)
            + rq[1, index].astype(jnp.float32)
            + rq[2, index].astype(jnp.float32)
        ).astype(q_out.dtype)

    q_out[:, group(c)] = total(dq[0, c], c)
    q_out[:, group(o)] = total(rq[0, o], o)


def per_device(
    queries,
    key_rows,
    value_rows,
    out_grad,
    logsumexp,
    out_dot,
    text_keys,
    text_values,
    text_length,
    window_reach,
):
    shape = queries.shape
    hidden = shape[3]
    rows = shape[0] * shape[1] * shape[2]
    head_count = logsumexp.shape[3]
    size = hidden // head_count
    heads = head_count // 2
    cols = heads * size
    tiles = lax.axis_size("ta")
    half = lax.axis_index("ha") % 2

    def stat(values):
        turned = values.reshape(rows, head_count).T.reshape(2, heads, rows)
        return jnp.pad(turned, ((0, 0), (0, 8 - heads), (0, 0)))

    stats = jnp.concatenate([stat(logsumexp * LOG2E), stat(out_dot)], axis=1)
    empty = jnp.zeros_like(stats)
    stats = jnp.where(
        half == 0,
        jnp.concatenate([stats, empty], axis=2),
        jnp.concatenate([empty, stats], axis=2),
    )
    text_k = lax.all_gather(text_keys, "ta", axis=0, tiled=True)
    text_v = lax.all_gather(text_values, "ta", axis=0, tiled=True)
    text_count = text_k.shape[0]
    vmem = pl.BlockSpec(memory_space=pltpu.VMEM)
    smem = pl.BlockSpec(memory_space=pltpu.SMEM)
    bf16, f32 = jnp.bfloat16, jnp.float32
    dma = pltpu.SemaphoreType.DMA
    query_grad, key_grad, value_grad, key_text, value_text = pl.pallas_call(
        functools.partial(kernel, tiles, heads, size),
        out_shape=[jax.ShapeDtypeStruct((rows, hidden), bf16)] * 3
        + [jax.ShapeDtypeStruct((text_count, cols), f32)] * 2,
        in_specs=[vmem] * 7 + [smem] * 2,
        out_specs=[vmem] * 5,
        scratch_shapes=[
            pltpu.VMEM((3, 2, rows, cols), bf16),
            pltpu.VMEM((3, 2, rows, cols), bf16),
            pltpu.VMEM((2, rows, cols), bf16),
            pltpu.VMEM((2, rows, cols), bf16),
            pltpu.VMEM((3, 2, 16, 2 * rows), f32),
            pltpu.VMEM((3, 16, 2 * rows), f32),
            pltpu.VMEM((2 * rows, cols), f32),
            pltpu.VMEM((2 * rows, cols), f32),
            pltpu.VMEM((3, 2, rows, cols), bf16),
            pltpu.VMEM((2, 2, rows, cols), bf16),
            pltpu.VMEM((3, 2, rows, cols), bf16),
            pltpu.VMEM((2, rows, cols), bf16),
            dma((4,)),
            dma((4,)),
            dma((4,)),
            dma((3, 2)),
            dma((3, 2)),
            dma((2, 2, 2, heads)),
            dma((2, 2, 2, heads)),
            dma((3, 2, heads)),
            dma((3, 2, heads)),
            dma((2, heads)),
            dma((2, heads)),
        ],
        compiler_params=pltpu.CompilerParams(
            collective_id=0, has_side_effects=True, vmem_limit_bytes=48 * 1024 * 1024
        ),
        cost_estimate=pl.CostEstimate(
            flops=20 * rows * rows * 7 * hidden, bytes_accessed=16 * rows * hidden, transcendentals=0
        ),
    )(
        queries.reshape(rows, hidden),
        out_grad.reshape(rows, hidden),
        key_rows.reshape(rows, hidden),
        value_rows.reshape(rows, hidden),
        stats,
        text_k,
        text_v,
        text_length,
        window_reach,
    )

    def text_total(part):
        whole = jnp.zeros((2, text_count, cols), f32)
        whole = lax.dynamic_update_slice_in_dim(whole, part[None], half, 0)
        whole = whole.transpose(1, 0, 2).reshape(text_count, hidden)
        return lax.psum_scatter(whole, "ta", scatter_dimension=0, tiled=True)

    totals = lax.psum((text_total(key_text), text_total(value_text)), "ha")
    return (
        query_grad.reshape(shape),
        key_grad.reshape(shape),
        value_grad.reshape(shape),
        totals[0].astype(bf16),
        totals[1].astype(bf16),
    )


def solution(mesh):
    block = P(("grp", "ta"), "ha", None, None)
    text = P(("grp", "ta"), None)
    return jax.shard_map(
        per_device,
        mesh=mesh,
        in_specs=(block,) * 6 + (text, text, P("grp"), P()),
        out_specs=(block,) * 3 + (text, text),
        check_vma=False,
    )
```

```python
import functools

import jax
import jax.numpy as jnp
from jax import lax
from jax.experimental import pallas as pl
from jax.experimental.pallas import tpu as pltpu
from jax.sharding import PartitionSpec as P

LOG2E = 1.4426950408889634
HIDDEN_LSE = 1e30
MESH_ID = pl.DeviceIdType.MESH
NT = (((1,), (1,)), ((), ()))
NN = (((1,), (0,)), ((), ()))
TN = (((0,), (0,)), ((), ()))


def dot(a, b, dims):
    return lax.dot_general(a, b, dims, preferred_element_type=jnp.float32)


def kernel(
    tiles,
    heads,
    size,
    fused,
    q_in,
    g_in,
    k_in,
    v_in,
    stat_in,
    text_k,
    text_v,
    length,
    reach,
    q_out,
    k_out,
    v_out,
    tk_out,
    tv_out,
    qw,
    gw,
    kw,
    vw,
    sw,
    st,
    ak,
    av,
    dq,
    dk,
    rq,
    rk,
    local_sem,
    pair_send,
    pair_recv,
    stat_send,
    stat_recv,
    far_send,
    far_recv,
    term_send,
    term_recv,
    kv_send,
    kv_recv,
    aq,
    *text_scratch,
):
    rows = q_in.shape[0]
    cols = heads * size
    scaling = size ** (-0.5)
    grp = lax.axis_index("grp")
    t = lax.axis_index("ta")
    ha = lax.axis_index("ha")
    c = lax.rem(ha, 2)
    o = 1 - c
    base = ha - c
    partner = (grp, t, base + o)
    has = (t > 0, t < tiles - 1)
    near = (t - 1, t + 1)

    def group(index):
        return pl.ds(pl.multiple_of(index * cols, 128), cols)

    def head(j):
        return pl.ds(pl.multiple_of(j * size, 128), size)

    def group_head(index, j):
        return pl.ds(pl.multiple_of(index * cols + j * size, 128), size)

    barrier = pltpu.get_barrier_semaphore()
    pl.semaphore_signal(barrier, inc=1, device_id=partner, device_id_type=MESH_ID)
    for d in range(2):

        @pl.when(has[d])
        def _():
            for cc in range(2):
                pl.semaphore_signal(
                    barrier, inc=1, device_id=(grp, near[d], base + cc), device_id_type=MESH_ID
                )

    count = 1 + 2 * jnp.where(t > 0, 1, 0) + 2 * jnp.where(t < tiles - 1, 1, 0)
    if fused:
        (tw, tp, tb, tr, tf, tsb, tz, tfb, to) = text_scratch[:9]
        (tg_send, tg_recv, tx_send, tx_recv, xr_sem, zt_send, zt_recv, fin_send, fin_recv) = (
            text_scratch[9:]
        )
        half_rows = tw.shape[3]
        p = lax.div(ha, 2)
        across = (grp, t, lax.rem(ha + 2, 4))
        diagonal = (grp, t, 2 * (1 - p) + o)
        for place in (across, diagonal):
            pl.semaphore_signal(barrier, inc=1, device_id=place, device_id_type=MESH_ID)
        for tt in range(tiles):

            @pl.when((t - tt) * (t - tt) > 1)
            def _():
                pl.semaphore_signal(
                    barrier, inc=1, device_id=(grp, tt, ha), device_id_type=MESH_ID
                )

        count = tiles + 2 + jnp.where(t > 0, 1, 0) + jnp.where(t < tiles - 1, 1, 0)
    pl.semaphore_wait(barrier, count)

    def elsewhere(action):
        for tt in range(tiles):

            @pl.when(t != tt)
            def _():
                action(tt)

    if fused:

        def text_gather(a, tt):
            return pltpu.make_async_remote_copy(
                src_ref=(text_k, text_v)[a].at[
                    pl.ds(pl.multiple_of(p * half_rows, half_rows), half_rows), group(c)
                ],
                dst_ref=tw.at[t, p, a],
                send_sem=tg_send.at[a, tt],
                recv_sem=tg_recv.at[a, t],
                device_id=(grp, tt, ha),
                device_id_type=MESH_ID,
            )

        def text_across(tt):
            return pltpu.make_async_remote_copy(
                src_ref=tw.at[tt, p],
                dst_ref=tw.at[tt, p],
                send_sem=tx_send.at[tt],
                recv_sem=tx_recv.at[tt],
                device_id=across,
                device_id_type=MESH_ID,
            )

        sum_across = pltpu.make_async_remote_copy(
            src_ref=tb.at[1 - p],
            dst_ref=tr,
            send_sem=xr_sem.at[0],
            recv_sem=xr_sem.at[1],
            device_id=across,
            device_id_type=MESH_ID,
        )

        def sum_along(tt):
            return pltpu.make_async_remote_copy(
                src_ref=tsb.at[tt],
                dst_ref=tz.at[t],
                send_sem=zt_send.at[tt],
                recv_sem=zt_recv.at[t],
                device_id=(grp, tt, ha),
                device_id_type=MESH_ID,
            )

        def spread(k):
            return pltpu.make_async_remote_copy(
                src_ref=tfb,
                dst_ref=to.at[c, p],
                send_sem=fin_send.at[k],
                recv_sem=fin_recv.at[c, p],
                device_id=(partner, across, diagonal)[k],
                device_id_type=MESH_ID,
            )

        def arrival(ref, sem):
            pltpu.make_async_copy(ref, ref, sem).wait()

    def far(d, cc, a, j):
        src = (q_in, g_in)[a]
        dst = (qw, gw)[a]
        return pltpu.make_async_remote_copy(
            src_ref=src.at[:, group_head(cc, j)],
            dst_ref=dst.at[2 - d, c, :, head(j)],
            send_sem=far_send.at[d, cc, a, j],
            recv_sem=far_recv.at[1 - d, c, a, j],
            device_id=(grp, near[d], base + cc),
            device_id_type=MESH_ID,
        )

    def far_wait(d, b, a, j):
        dst = (qw, gw)[a].at[1 + d, b, :, head(j)]
        pltpu.make_async_copy(dst, dst, far_recv.at[d, b, a, j]).wait()

    def stat_far(d, cc):
        return pltpu.make_async_remote_copy(
            src_ref=stat_in.at[cc],
            dst_ref=sw.at[2 - d, c],
            send_sem=stat_send.at[1 + d, cc],
            recv_sem=stat_recv.at[2 - d, c],
            device_id=(grp, near[d], base + cc),
            device_id_type=MESH_ID,
        )

    def pair(a):
        src = (q_in, g_in, k_in, v_in)[a]
        dst = (qw.at[0, c], gw.at[0, c], kw.at[c], vw.at[c])[a]
        return pltpu.make_async_remote_copy(
            src_ref=src.at[:, group(o)],
            dst_ref=dst,
            send_sem=pair_send.at[a],
            recv_sem=pair_recv.at[a],
            device_id=partner,
            device_id_type=MESH_ID,
        )

    def own(a):
        src = (q_in, g_in, k_in, v_in)[a]
        dst = (qw.at[0, c], gw.at[0, c], kw.at[c], vw.at[c])[a]
        return pltpu.make_async_copy(src.at[:, group(c)], dst, local_sem.at[a])

    stat_pair = pltpu.make_async_remote_copy(
        src_ref=stat_in.at[o],
        dst_ref=sw.at[0, c],
        send_sem=stat_send.at[0, 0],
        recv_sem=stat_recv.at[0, 0],
        device_id=partner,
        device_id_type=MESH_ID,
    )

    stat_pair.start()
    if fused:

        def send_text(tt):
            for a in range(2):
                text_gather(a, tt).start()

        elsewhere(send_text)
    for a in range(4):
        pair(a).start()
        own(a).start()
    for d in range(2):

        @pl.when(has[d])
        def _():
            for cc in range(2):
                stat_far(d, cc).start()

    def send_far(j, carry):
        for d in range(2):

            @pl.when(has[d])
            def _():
                for a in range(2):
                    for cc in range(2):
                        far(d, cc, a, j).start()

        return carry

    lax.fori_loop(0, heads, send_far, 0)

    for d in range(2):

        @pl.when(jnp.logical_not(has[d]))
        def _():
            rq[1 + d] = jnp.zeros_like(rq[1 + d])

    if fused:
        for hh in range(2):
            for a in range(2):
                tw[t, hh, a] = (text_k, text_v)[a][hh * half_rows : (hh + 1) * half_rows, group(c)]

        def forward_text(tt):
            for a in range(2):
                arrival(tw.at[tt, p, a], tg_recv.at[a, tt])
            text_across(tt).start()

        elsewhere(forward_text)

    for a in range(4):
        own(a).wait()
        pair(a).wait_recv()
    stat_pair.wait_recv()
    st[0] = stat_in[c] + sw[0, o]

    def term(s, b, j):
        target = partner if s == 0 else (grp, near[s - 1], base + b)
        slot = (0, 2, 1)[s]
        return pltpu.make_async_remote_copy(
            src_ref=dq.at[s, b, :, head(j)],
            dst_ref=rq.at[slot, c, :, head(j)],
            send_sem=term_send.at[s, 0 if s == 0 else b, j],
            recv_sem=term_recv.at[slot, c, j],
            device_id=target,
            device_id_type=MESH_ID,
        )

    def term_wait(slot, group_index, j):
        dst = rq.at[slot, group_index, :, head(j)]
        pltpu.make_async_copy(dst, dst, term_recv.at[slot, group_index, j]).wait()

    def kv(a, j):
        return pltpu.make_async_remote_copy(
            src_ref=dk.at[a, o, :, head(j)],
            dst_ref=rk.at[a, :, head(j)],
            send_sem=kv_send.at[a, j],
            recv_sem=kv_recv.at[a, j],
            device_id=partner,
            device_id_type=MESH_ID,
        )

    def both(ref, j):
        return ref[:, :, head(j)].reshape(2 * rows, size)

    def grads(q, g, k, v, lse, out_dot, ok):
        weight = jnp.exp2(dot(k, q, NT) * (scaling * LOG2E) - lse)
        if ok is not None:
            weight = jnp.where(ok, weight, 0.0)
        score = (weight * (dot(v, g, NT) - out_dot) * scaling).astype(jnp.bfloat16)
        prob = weight.astype(jnp.bfloat16)
        return dot(score, k, TN), dot(score, q, NN), dot(prob, g, NN)

    text_count = tiles * text_k.shape[0] if fused else text_k.shape[0]
    text_ok = lax.broadcasted_iota(jnp.int32, (text_count, 1), 0) < length[0]

    def stats(s, j):
        return st[s, pl.ds(j, 1), :], st[s, pl.ds(8 + j, 1), :]

    def near_step(j, carry):
        q, g = both(qw.at[0], j), both(gw.at[0], j)
        lse, out_dot = stats(0, j)
        dq_own, dk_own, dv_own = grads(q, g, both(kw, j), both(vw, j), lse, out_dot, None)
        ak[:, head(j)] = dk_own
        av[:, head(j)] = dv_own
        aq[:, head(j)] = dq_own
        return carry

    def text_step(j, carry):
        q, g = both(qw.at[0], j), both(gw.at[0], j)
        lse, out_dot = stats(0, j)
        if fused:
            tk = tw[:, :, 0, :, head(j)].reshape(text_count, size)
            tv = tw[:, :, 1, :, head(j)].reshape(text_count, size)
        else:
            tk, tv = text_k[:, group_head(c, j)], text_v[:, group_head(c, j)]
        dq_text, dk_text, dv_text = grads(q, g, tk, tv, lse, out_dot, text_ok)
        if fused:
            for a, part in enumerate((dk_text, dv_text)):
                for tt in range(tiles):
                    for hh in range(2):
                        low = (2 * tt + hh) * half_rows
                        piece = part[low : low + half_rows]
                        tp[hh, tt, a, :, head(j)] = piece
                        tb[hh, tt, a, :, head(j)] = piece.astype(jnp.bfloat16)
        else:
            tk_out[:, head(j)] = dk_text
            tv_out[:, head(j)] = dv_text
        total = (aq[:, head(j)] + dq_text).astype(jnp.bfloat16)
        dq[0, :, :, head(j)] = total.reshape(2, rows, size)
        term(0, o, j).start()
        return carry

    lax.fori_loop(0, heads, near_step, 0)
    if fused:
        elsewhere(lambda tt: arrival(tw.at[tt, 1 - p], tx_recv.at[tt]))
    lax.fori_loop(0, heads, text_step, 0)
    if fused:
        sum_across.start()

    for d in range(2):

        @pl.when(has[d])
        def _():
            for b in range(2):
                dst = sw.at[1 + d, b]
                pltpu.make_async_copy(dst, dst, stat_recv.at[1 + d, b]).wait()
            st[1 + d] = sw[1 + d, 0] + sw[1 + d, 1]

    def far_step(j, carry):
        for d in range(2):

            @pl.when(has[d])
            def _():
                for a in range(2):
                    for b in range(2):
                        far_wait(d, b, a, j)
                seen = reach[c * heads + j, 1 - d] >= 1
                lse = st[1 + d, pl.ds(j, 1), :] + jnp.where(seen, 0.0, HIDDEN_LSE)
                out_dot = st[1 + d, pl.ds(8 + j, 1), :]
                dq_far, dk_far, dv_far = grads(
                    both(qw.at[1 + d], j),
                    both(gw.at[1 + d], j),
                    both(kw, j),
                    both(vw, j),
                    lse,
                    out_dot,
                    None,
                )
                ak[:, head(j)] += dk_far
                av[:, head(j)] += dv_far
                dq[1 + d, :, :, head(j)] = (
                    dq_far.astype(jnp.bfloat16).reshape(2, rows, size)
                )
                for b in range(2):
                    term(1 + d, b, j).start()

        dk[0, :, :, head(j)] = (
            ak[:, head(j)].astype(jnp.bfloat16).reshape(2, rows, size)
        )
        dk[1, :, :, head(j)] = av[:, head(j)].astype(jnp.bfloat16).reshape(2, rows, size)
        for a in range(2):
            kv(a, j).start()
        return carry

    early = 2
    lax.fori_loop(0, early, far_step, 0)
    if fused:
        sum_across.wait_recv()
        for tt in range(tiles):
            tsb[tt] = (tp[p, tt] + tr[tt].astype(jnp.float32)).astype(jnp.bfloat16)
        tf[...] = tp[p, t] + tr[t].astype(jnp.float32)
        elsewhere(lambda tt: sum_along(tt).start())
    lax.fori_loop(early, heads, far_step, 0)
    if fused:

        def add_sum(tt):
            arrival(tz.at[tt], zt_recv.at[tt])
            tf[...] += tz[tt].astype(jnp.float32)

        elsewhere(add_sum)
        tfb[...] = tf[...].astype(jnp.bfloat16)
        for k in range(3):
            spread(k).start()
        to[c, p] = tfb[...]

    k_out[:, group(c)] = dk[0, c]
    v_out[:, group(c)] = dk[1, c]

    def finish(j, carry):
        for a in range(2):
            kv(a, j).wait()
        term(0, o, j).wait_send()
        term_wait(0, o, j)
        for d in range(2):

            @pl.when(has[d])
            def _():
                for b in range(2):
                    term_wait(1 + d, b, j)
                    term(1 + d, b, j).wait_send()
                    for a in range(2):
                        far(d, b, a, j).wait_send()

        return carry

    lax.fori_loop(0, heads, finish, 0)
    stat_pair.wait_send()
    for a in range(4):
        pair(a).wait_send()
    for d in range(2):

        @pl.when(has[d])
        def _():
            for cc in range(2):
                stat_far(d, cc).wait_send()

    if fused:
        for cc, pp in ((o, p), (c, 1 - p), (o, 1 - p)):
            arrival(to.at[cc, pp], fin_recv.at[cc, pp])
        for hh in range(2):
            for cc in range(2):
                spot = pl.ds(hh * half_rows, half_rows), pl.ds(cc * cols, cols)
                tk_out[spot] = to[cc, hh, 0]
                tv_out[spot] = to[cc, hh, 1]
        for k in range(3):
            spread(k).wait_send()
        sum_across.wait_send()

        def end_text(tt):
            for a in range(2):
                text_gather(a, tt).wait_send()
            text_across(tt).wait_send()
            sum_along(tt).wait_send()

        elsewhere(end_text)

    k_out[:, group(o)] = rk[0]
    v_out[:, group(o)] = rk[1]

    def total(own_part, index):
        return (
            own_part.astype(jnp.float32)
            + rq[1, index].astype(jnp.float32)
            + rq[2, index].astype(jnp.float32)
        ).astype(q_out.dtype)

    q_out[:, group(c)] = total(dq[0, c], c)
    q_out[:, group(o)] = total(rq[0, o], o)


def per_device(
    queries,
    key_rows,
    value_rows,
    out_grad,
    logsumexp,
    out_dot,
    text_keys,
    text_values,
    text_length,
    window_reach,
):
    shape = queries.shape
    hidden = shape[3]
    rows = shape[0] * shape[1] * shape[2]
    head_count = logsumexp.shape[3]
    size = hidden // head_count
    heads = head_count // 2
    cols = heads * size
    tiles = lax.axis_size("ta")
    half = lax.axis_index("ha") % 2

    def stat(values):
        turned = values.reshape(rows, head_count).T.reshape(2, heads, rows)
        return jnp.pad(turned, ((0, 0), (0, 8 - heads), (0, 0)))

    stats = jnp.concatenate([stat(logsumexp * LOG2E), stat(out_dot)], axis=1)
    empty = jnp.zeros_like(stats)
    stats = jnp.where(
        half == 0,
        jnp.concatenate([stats, empty], axis=2),
        jnp.concatenate([empty, stats], axis=2),
    )
    text_rows = text_keys.shape[0]
    text_count = tiles * text_rows
    half_rows = text_rows // 2
    fused = lax.axis_size("ha") == 4 and text_rows % 32 == 0
    bf16, f32 = jnp.bfloat16, jnp.float32
    dma = pltpu.SemaphoreType.DMA
    if fused:
        text_k, text_v = text_keys, text_values
        text_out = jax.ShapeDtypeStruct((text_rows, hidden), bf16)
        text_scratch = [
            pltpu.VMEM((tiles, 2, 2, half_rows, cols), bf16),
            pltpu.VMEM((2, tiles, 2, half_rows, cols), f32),
            pltpu.VMEM((2, tiles, 2, half_rows, cols), bf16),
            pltpu.VMEM((tiles, 2, half_rows, cols), bf16),
            pltpu.VMEM((2, half_rows, cols), f32),
            pltpu.VMEM((tiles, 2, half_rows, cols), bf16),
            pltpu.VMEM((tiles, 2, half_rows, cols), bf16),
            pltpu.VMEM((2, half_rows, cols), bf16),
            pltpu.VMEM((2, 2, 2, half_rows, cols), bf16),
            dma((2, tiles)),
            dma((2, tiles)),
            dma((tiles,)),
            dma((tiles,)),
            dma((2,)),
            dma((tiles,)),
            dma((tiles,)),
            dma((3,)),
            dma((2, 2)),
        ]
    else:
        text_k = lax.all_gather(text_keys, "ta", axis=0, tiled=True)
        text_v = lax.all_gather(text_values, "ta", axis=0, tiled=True)
        text_out = jax.ShapeDtypeStruct((text_count, cols), f32)
        text_scratch = []
    vmem = pl.BlockSpec(memory_space=pltpu.VMEM)
    smem = pl.BlockSpec(memory_space=pltpu.SMEM)
    query_grad, key_grad, value_grad, key_text, value_text = pl.pallas_call(
        functools.partial(kernel, tiles, heads, size, fused),
        out_shape=[jax.ShapeDtypeStruct((rows, hidden), bf16)] * 3
        + [text_out] * 2,
        in_specs=[vmem] * 7 + [smem] * 2,
        out_specs=[vmem] * 5,
        scratch_shapes=[
            pltpu.VMEM((3, 2, rows, cols), bf16),
            pltpu.VMEM((3, 2, rows, cols), bf16),
            pltpu.VMEM((2, rows, cols), bf16),
            pltpu.VMEM((2, rows, cols), bf16),
            pltpu.VMEM((3, 2, 16, 2 * rows), f32),
            pltpu.VMEM((3, 16, 2 * rows), f32),
            pltpu.VMEM((2 * rows, cols), f32),
            pltpu.VMEM((2 * rows, cols), f32),
            pltpu.VMEM((3, 2, rows, cols), bf16),
            pltpu.VMEM((2, 2, rows, cols), bf16),
            pltpu.VMEM((3, 2, rows, cols), bf16),
            pltpu.VMEM((2, rows, cols), bf16),
            dma((4,)),
            dma((4,)),
            dma((4,)),
            dma((3, 2)),
            dma((3, 2)),
            dma((2, 2, 2, heads)),
            dma((2, 2, 2, heads)),
            dma((3, 2, heads)),
            dma((3, 2, heads)),
            dma((2, heads)),
            dma((2, heads)),
            pltpu.VMEM((2 * rows, cols), f32),
        ]
        + text_scratch,
        compiler_params=pltpu.CompilerParams(
            collective_id=0, has_side_effects=True, vmem_limit_bytes=48 * 1024 * 1024
        ),
        cost_estimate=pl.CostEstimate(
            flops=20 * rows * rows * 7 * hidden, bytes_accessed=16 * rows * hidden, transcendentals=0
        ),
    )(
        queries.reshape(rows, hidden),
        out_grad.reshape(rows, hidden),
        key_rows.reshape(rows, hidden),
        value_rows.reshape(rows, hidden),
        stats,
        text_k,
        text_v,
        text_length,
        window_reach,
    )

    grads = tuple(grad.reshape(shape) for grad in (query_grad, key_grad, value_grad))
    if fused:
        return grads + (key_text, value_text)

    def text_total(part):
        whole = jnp.zeros((2, text_count, cols), f32)
        whole = lax.dynamic_update_slice_in_dim(whole, part[None], half, 0)
        whole = whole.transpose(1, 0, 2).reshape(text_count, hidden)
        return lax.psum_scatter(whole, "ta", scatter_dimension=0, tiled=True)

    totals = lax.psum((text_total(key_text), text_total(value_text)), "ha")
    return grads + (totals[0].astype(bf16), totals[1].astype(bf16))


def solution(mesh):
    block = P(("grp", "ta"), "ha", None, None)
    text = P(("grp", "ta"), None)
    return jax.shard_map(
        per_device,
        mesh=mesh,
        in_specs=(block,) * 6 + (text, text, P("grp"), P()),
        out_specs=(block,) * 3 + (text, text),
        check_vma=False,
    )
```

```python
import functools

import jax
import jax.numpy as jnp
from jax import lax
from jax.experimental import pallas as pl
from jax.experimental.pallas import tpu as pltpu
from jax.sharding import PartitionSpec as P

LOG2E = 1.4426950408889634
HIDDEN_LSE = 1e30
MESH_ID = pl.DeviceIdType.MESH
NT = (((1,), (1,)), ((), ()))
NN = (((1,), (0,)), ((), ()))
TN = (((0,), (0,)), ((), ()))


def dot(a, b, dims):
    return lax.dot_general(a, b, dims, preferred_element_type=jnp.float32)


def kernel(
    tiles,
    heads,
    size,
    fused,
    q_in,
    g_in,
    k_in,
    v_in,
    stat_in,
    text_k,
    text_v,
    length,
    reach,
    q_out,
    k_out,
    v_out,
    tk_out,
    tv_out,
    qw,
    gw,
    kw,
    vw,
    sw,
    st,
    ak,
    av,
    dq,
    dk,
    rq,
    rk,
    local_sem,
    pair_send,
    pair_recv,
    stat_send,
    stat_recv,
    far_send,
    far_recv,
    term_send,
    term_recv,
    kv_send,
    kv_recv,
    aq,
    qs,
    out_sem,
    *text_scratch,
):
    rows = q_in.shape[0]
    cols = heads * size
    scaling = size ** (-0.5)
    grp = lax.axis_index("grp")
    t = lax.axis_index("ta")
    ha = lax.axis_index("ha")
    c = lax.rem(ha, 2)
    o = 1 - c
    base = ha - c
    partner = (grp, t, base + o)
    has = (t > 0, t < tiles - 1)
    near = (t - 1, t + 1)

    def group(index):
        return pl.ds(pl.multiple_of(index * cols, 128), cols)

    def head(j):
        return pl.ds(pl.multiple_of(j * size, 128), size)

    def group_head(index, j):
        return pl.ds(pl.multiple_of(index * cols + j * size, 128), size)

    barrier = pltpu.get_barrier_semaphore()
    pl.semaphore_signal(barrier, inc=1, device_id=partner, device_id_type=MESH_ID)
    for d in range(2):

        @pl.when(has[d])
        def _():
            for cc in range(2):
                pl.semaphore_signal(
                    barrier, inc=1, device_id=(grp, near[d], base + cc), device_id_type=MESH_ID
                )

    count = 1 + 2 * jnp.where(t > 0, 1, 0) + 2 * jnp.where(t < tiles - 1, 1, 0)
    if fused:
        (tw, tp, tb, tr, tf, tsb, tz, tfb, to) = text_scratch[:9]
        (tg_send, tg_recv, tx_send, tx_recv, xr_sem, zt_send, zt_recv, fin_send, fin_recv) = (
            text_scratch[9:18]
        )
        tl_sem = text_scratch[18]
        half_rows = tw.shape[3]
        p = lax.div(ha, 2)
        across = (grp, t, lax.rem(ha + 2, 4))
        diagonal = (grp, t, 2 * (1 - p) + o)
        for place in (across, diagonal):
            pl.semaphore_signal(barrier, inc=1, device_id=place, device_id_type=MESH_ID)
        for tt in range(tiles):

            @pl.when((t - tt) * (t - tt) > 1)
            def _():
                pl.semaphore_signal(
                    barrier, inc=1, device_id=(grp, tt, ha), device_id_type=MESH_ID
                )

        count = tiles + 2 + jnp.where(t > 0, 1, 0) + jnp.where(t < tiles - 1, 1, 0)
    pl.semaphore_wait(barrier, count)

    def elsewhere(action):
        for tt in range(tiles):

            @pl.when(t != tt)
            def _():
                action(tt)

    if fused:

        def text_gather(a, tt):
            return pltpu.make_async_remote_copy(
                src_ref=(text_k, text_v)[a].at[
                    pl.ds(pl.multiple_of(p * half_rows, half_rows), half_rows), group(c)
                ],
                dst_ref=tw.at[t, p, a],
                send_sem=tg_send.at[a, tt],
                recv_sem=tg_recv.at[a, t],
                device_id=(grp, tt, ha),
                device_id_type=MESH_ID,
            )

        def text_own(a, hh):
            return pltpu.make_async_copy(
                (text_k, text_v)[a].at[pl.ds(hh * half_rows, half_rows), group(c)],
                tw.at[t, hh, a],
                tl_sem.at[a, hh],
            )

        def text_across(tt):
            return pltpu.make_async_remote_copy(
                src_ref=tw.at[tt, p],
                dst_ref=tw.at[tt, p],
                send_sem=tx_send.at[tt],
                recv_sem=tx_recv.at[tt],
                device_id=across,
                device_id_type=MESH_ID,
            )

        sum_across = pltpu.make_async_remote_copy(
            src_ref=tb.at[1 - p],
            dst_ref=tr,
            send_sem=xr_sem.at[0],
            recv_sem=xr_sem.at[1],
            device_id=across,
            device_id_type=MESH_ID,
        )

        def sum_along(tt):
            return pltpu.make_async_remote_copy(
                src_ref=tsb.at[tt],
                dst_ref=tz.at[t],
                send_sem=zt_send.at[tt],
                recv_sem=zt_recv.at[t],
                device_id=(grp, tt, ha),
                device_id_type=MESH_ID,
            )

        def spread(k):
            return pltpu.make_async_remote_copy(
                src_ref=tfb,
                dst_ref=to.at[c, p],
                send_sem=fin_send.at[k],
                recv_sem=fin_recv.at[c, p],
                device_id=(partner, across, diagonal)[k],
                device_id_type=MESH_ID,
            )

        def arrival(ref, sem):
            pltpu.make_async_copy(ref, ref, sem).wait()

    def far(d, cc, a, j):
        src = (q_in, g_in)[a]
        dst = (qw, gw)[a]
        return pltpu.make_async_remote_copy(
            src_ref=src.at[:, group_head(cc, j)],
            dst_ref=dst.at[2 - d, c, :, head(j)],
            send_sem=far_send.at[d, cc, a, j],
            recv_sem=far_recv.at[1 - d, c, a, j],
            device_id=(grp, near[d], base + cc),
            device_id_type=MESH_ID,
        )

    def far_wait(d, b, a, j):
        dst = (qw, gw)[a].at[1 + d, b, :, head(j)]
        pltpu.make_async_copy(dst, dst, far_recv.at[d, b, a, j]).wait()

    def stat_far(d, cc):
        return pltpu.make_async_remote_copy(
            src_ref=stat_in.at[cc],
            dst_ref=sw.at[2 - d, c],
            send_sem=stat_send.at[1 + d, cc],
            recv_sem=stat_recv.at[2 - d, c],
            device_id=(grp, near[d], base + cc),
            device_id_type=MESH_ID,
        )

    def pair(a):
        src = (q_in, g_in, k_in, v_in)[a]
        dst = (qw.at[0, c], gw.at[0, c], kw.at[c], vw.at[c])[a]
        return pltpu.make_async_remote_copy(
            src_ref=src.at[:, group(o)],
            dst_ref=dst,
            send_sem=pair_send.at[a],
            recv_sem=pair_recv.at[a],
            device_id=partner,
            device_id_type=MESH_ID,
        )

    def own(a):
        src = (q_in, g_in, k_in, v_in)[a]
        dst = (qw.at[0, c], gw.at[0, c], kw.at[c], vw.at[c])[a]
        return pltpu.make_async_copy(src.at[:, group(c)], dst, local_sem.at[a])

    stat_pair = pltpu.make_async_remote_copy(
        src_ref=stat_in.at[o],
        dst_ref=sw.at[0, c],
        send_sem=stat_send.at[0, 0],
        recv_sem=stat_recv.at[0, 0],
        device_id=partner,
        device_id_type=MESH_ID,
    )

    stat_pair.start()
    if fused:

        def send_text(tt):
            for a in range(2):
                text_gather(a, tt).start()

        elsewhere(send_text)
        for a in range(2):
            for hh in range(2):
                text_own(a, hh).start()
    for a in range(4):
        pair(a).start()
        own(a).start()
    for d in range(2):

        @pl.when(has[d])
        def _():
            for cc in range(2):
                stat_far(d, cc).start()

    def send_far(j, carry):
        for d in range(2):

            @pl.when(has[d])
            def _():
                for a in range(2):
                    for cc in range(2):
                        far(d, cc, a, j).start()

        return carry

    lax.fori_loop(0, heads, send_far, 0)

    for d in range(2):

        @pl.when(jnp.logical_not(has[d]))
        def _():
            rq[1 + d] = jnp.zeros_like(rq[1 + d])

    if fused:
        def forward_text(tt):
            for a in range(2):
                arrival(tw.at[tt, p, a], tg_recv.at[a, tt])
            text_across(tt).start()

        elsewhere(forward_text)

    for a in range(4):
        own(a).wait()
        pair(a).wait_recv()
    stat_pair.wait_recv()
    def fill(s, values):
        st[s, 0:8] = values[0:8] * LOG2E
        st[s, 8:16] = values[8:16]

    fill(0, stat_in[c] + sw[0, o])

    def term(s, b, j):
        target = partner if s == 0 else (grp, near[s - 1], base + b)
        slot = (0, 2, 1)[s]
        return pltpu.make_async_remote_copy(
            src_ref=dq.at[s, b, :, head(j)],
            dst_ref=rq.at[slot, c, :, head(j)],
            send_sem=term_send.at[s, 0 if s == 0 else b, j],
            recv_sem=term_recv.at[slot, c, j],
            device_id=target,
            device_id_type=MESH_ID,
        )

    def term_wait(slot, group_index, j):
        dst = rq.at[slot, group_index, :, head(j)]
        pltpu.make_async_copy(dst, dst, term_recv.at[slot, group_index, j]).wait()

    def kv(a, j):
        return pltpu.make_async_remote_copy(
            src_ref=dk.at[a, o, :, head(j)],
            dst_ref=rk.at[a, :, head(j)],
            send_sem=kv_send.at[a, j],
            recv_sem=kv_recv.at[a, j],
            device_id=partner,
            device_id_type=MESH_ID,
        )

    def both(ref, j):
        return ref[:, :, head(j)].reshape(2 * rows, size)

    def grads(q, g, k, v, lse, out_dot, ok):
        weight = jnp.exp2(dot(k, q, NT) * (scaling * LOG2E) - lse)
        if ok is not None:
            weight = jnp.where(ok, weight, 0.0)
        score = (weight * (dot(v, g, NT) - out_dot) * scaling).astype(jnp.bfloat16)
        prob = weight.astype(jnp.bfloat16)
        return dot(score, k, TN), dot(score, q, NN), dot(prob, g, NN)

    text_count = tiles * text_k.shape[0] if fused else text_k.shape[0]
    text_ok = lax.broadcasted_iota(jnp.int32, (text_count, 1), 0) < length[0]

    def stats(s, j):
        return st[s, pl.ds(j, 1), :], st[s, pl.ds(8 + j, 1), :]

    def near_step(j, carry):
        q, g = both(qw.at[0], j), both(gw.at[0], j)
        lse, out_dot = stats(0, j)
        dq_own, dk_own, dv_own = grads(q, g, both(kw, j), both(vw, j), lse, out_dot, None)
        ak[:, head(j)] = dk_own
        av[:, head(j)] = dv_own
        aq[:, head(j)] = dq_own
        return carry

    def text_step(j, carry):
        q, g = both(qw.at[0], j), both(gw.at[0], j)
        lse, out_dot = stats(0, j)
        if fused:
            tk = tw[:, :, 0, :, head(j)].reshape(text_count, size)
            tv = tw[:, :, 1, :, head(j)].reshape(text_count, size)
        else:
            tk, tv = text_k[:, group_head(c, j)], text_v[:, group_head(c, j)]
        dq_text, dk_text, dv_text = grads(q, g, tk, tv, lse, out_dot, text_ok)
        if fused:
            for a, part in enumerate((dk_text, dv_text)):
                for tt in range(tiles):
                    for hh in range(2):
                        low = (2 * tt + hh) * half_rows
                        piece = part[low : low + half_rows]
                        tp[hh, tt, a, :, head(j)] = piece
                        tb[hh, tt, a, :, head(j)] = piece.astype(jnp.bfloat16)
        else:
            tk_out[:, head(j)] = dk_text
            tv_out[:, head(j)] = dv_text
        total = (aq[:, head(j)] + dq_text).astype(jnp.bfloat16)
        dq[0, :, :, head(j)] = total.reshape(2, rows, size)
        term(0, o, j).start()
        return carry

    lax.fori_loop(0, heads, near_step, 0)
    if fused:
        elsewhere(lambda tt: arrival(tw.at[tt, 1 - p], tx_recv.at[tt]))
        for a in range(2):
            for hh in range(2):
                text_own(a, hh).wait()
    lax.fori_loop(0, heads, text_step, 0)
    if fused:
        sum_across.start()

    for d in range(2):

        @pl.when(has[d])
        def _():
            for b in range(2):
                dst = sw.at[1 + d, b]
                pltpu.make_async_copy(dst, dst, stat_recv.at[1 + d, b]).wait()
            fill(1 + d, sw[1 + d, 0] + sw[1 + d, 1])

    def far_step(j, carry):
        for d in range(2):

            @pl.when(has[d])
            def _():
                for a in range(2):
                    for b in range(2):
                        far_wait(d, b, a, j)
                seen = reach[1 - d, c * heads + j] >= 1
                lse = st[1 + d, pl.ds(j, 1), :] + jnp.where(seen, 0.0, HIDDEN_LSE)
                out_dot = st[1 + d, pl.ds(8 + j, 1), :]
                dq_far, dk_far, dv_far = grads(
                    both(qw.at[1 + d], j),
                    both(gw.at[1 + d], j),
                    both(kw, j),
                    both(vw, j),
                    lse,
                    out_dot,
                    None,
                )
                ak[:, head(j)] += dk_far
                av[:, head(j)] += dv_far
                dq[1 + d, :, :, head(j)] = (
                    dq_far.astype(jnp.bfloat16).reshape(2, rows, size)
                )
                for b in range(2):
                    term(1 + d, b, j).start()

        dk[0, :, :, head(j)] = (
            ak[:, head(j)].astype(jnp.bfloat16).reshape(2, rows, size)
        )
        dk[1, :, :, head(j)] = av[:, head(j)].astype(jnp.bfloat16).reshape(2, rows, size)
        for a in range(2):
            kv(a, j).start()
        return carry

    early = 2
    lax.fori_loop(0, early, far_step, 0)
    if fused:
        sum_across.wait_recv()
        for tt in range(tiles):
            tsb[tt] = (tp[p, tt] + tr[tt].astype(jnp.float32)).astype(jnp.bfloat16)
        tf[...] = tp[p, t] + tr[t].astype(jnp.float32)
        elsewhere(lambda tt: sum_along(tt).start())
    lax.fori_loop(early, heads, far_step, 0)
    if fused:

        def add_sum(tt):
            arrival(tz.at[tt], zt_recv.at[tt])
            tf[...] += tz[tt].astype(jnp.float32)

        elsewhere(add_sum)
        tfb[...] = tf[...].astype(jnp.bfloat16)
        for k in range(3):
            spread(k).start()
        to[c, p] = tfb[...]

    def put(a, index, source):
        return pltpu.make_async_copy(
            source, (k_out, v_out)[a].at[:, group(index)], out_sem.at[a, index]
        )

    for a in range(2):
        put(a, c, dk.at[a, c]).start()

    def finish_kv(j, carry):
        for a in range(2):
            kv(a, j).wait()
        return carry

    lax.fori_loop(0, heads, finish_kv, 0)
    for a in range(2):
        put(a, o, rk.at[a]).start()
    stat_pair.wait_send()
    for a in range(4):
        pair(a).wait_send()
    for d in range(2):

        @pl.when(has[d])
        def _():
            for cc in range(2):
                stat_far(d, cc).wait_send()

    if fused:
        for cc, pp in ((o, p), (c, 1 - p), (o, 1 - p)):
            arrival(to.at[cc, pp], fin_recv.at[cc, pp])
        for hh in range(2):
            for cc in range(2):
                spot = pl.ds(hh * half_rows, half_rows), pl.ds(cc * cols, cols)
                tk_out[spot] = to[cc, hh, 0]
                tv_out[spot] = to[cc, hh, 1]
        for k in range(3):
            spread(k).wait_send()
        sum_across.wait_send()

        def end_text(tt):
            for a in range(2):
                text_gather(a, tt).wait_send()
            text_across(tt).wait_send()
            sum_along(tt).wait_send()

        elsewhere(end_text)

    def total(own_part, index, j):
        return (
            own_part.astype(jnp.float32)
            + rq[1, index, :, head(j)].astype(jnp.float32)
            + rq[2, index, :, head(j)].astype(jnp.float32)
        ).astype(jnp.bfloat16)

    def put_query(index, j):
        return pltpu.make_async_copy(
            qs.at[index, :, head(j)],
            q_out.at[:, group_head(index, j)],
            out_sem.at[2 + index, j],
        )

    def finish(j, carry):
        term(0, o, j).wait_send()
        term_wait(0, o, j)
        for d in range(2):

            @pl.when(has[d])
            def _():
                for b in range(2):
                    for a in range(2):
                        far(d, b, a, j).wait_send()
                    term_wait(1 + d, b, j)

        qs[c, :, head(j)] = total(dq[0, c, :, head(j)], c, j)
        qs[o, :, head(j)] = total(rq[0, o, :, head(j)], o, j)
        for index in range(2):
            put_query(index, j).start()
        return carry

    lax.fori_loop(0, heads, finish, 0)

    def finish_send(j, carry):
        for d in range(2):

            @pl.when(has[d])
            def _():
                for b in range(2):
                    term(1 + d, b, j).wait_send()

        for index in range(2):
            put_query(index, j).wait()
        return carry

    lax.fori_loop(0, heads, finish_send, 0)
    for a in range(2):
        put(a, c, dk.at[a, c]).wait()
        put(a, o, rk.at[a]).wait()


def per_device(
    queries,
    key_rows,
    value_rows,
    out_grad,
    logsumexp,
    out_dot,
    text_keys,
    text_values,
    text_length,
    window_reach,
):
    shape = queries.shape
    hidden = shape[3]
    rows = shape[0] * shape[1] * shape[2]
    head_count = logsumexp.shape[3]
    size = hidden // head_count
    heads = head_count // 2
    cols = heads * size
    tiles = lax.axis_size("ta")
    half = lax.axis_index("ha") % 2

    def stat(values):
        turned = values.reshape(rows, head_count).T.reshape(2, heads, rows)
        return jnp.pad(turned, ((0, 0), (0, 8 - heads), (0, 0)))

    stats = jnp.concatenate([stat(logsumexp), stat(out_dot)], axis=1)
    empty = jnp.zeros_like(stats)
    stats = jnp.where(
        half == 0,
        jnp.concatenate([stats, empty], axis=2),
        jnp.concatenate([empty, stats], axis=2),
    )
    text_rows = text_keys.shape[0]
    text_count = tiles * text_rows
    half_rows = text_rows // 2
    fused = lax.axis_size("ha") == 4 and text_rows % 32 == 0
    bf16, f32 = jnp.bfloat16, jnp.float32
    dma = pltpu.SemaphoreType.DMA
    if fused:
        text_k, text_v = text_keys, text_values
        text_out = jax.ShapeDtypeStruct((text_rows, hidden), bf16)
        text_scratch = [
            pltpu.VMEM((tiles, 2, 2, half_rows, cols), bf16),
            pltpu.VMEM((2, tiles, 2, half_rows, cols), f32),
            pltpu.VMEM((2, tiles, 2, half_rows, cols), bf16),
            pltpu.VMEM((tiles, 2, half_rows, cols), bf16),
            pltpu.VMEM((2, half_rows, cols), f32),
            pltpu.VMEM((tiles, 2, half_rows, cols), bf16),
            pltpu.VMEM((tiles, 2, half_rows, cols), bf16),
            pltpu.VMEM((2, half_rows, cols), bf16),
            pltpu.VMEM((2, 2, 2, half_rows, cols), bf16),
            dma((2, tiles)),
            dma((2, tiles)),
            dma((tiles,)),
            dma((tiles,)),
            dma((2,)),
            dma((tiles,)),
            dma((tiles,)),
            dma((3,)),
            dma((2, 2)),
            dma((2, 2)),
        ]
    else:
        text_k = lax.all_gather(text_keys, "ta", axis=0, tiled=True)
        text_v = lax.all_gather(text_values, "ta", axis=0, tiled=True)
        text_out = jax.ShapeDtypeStruct((text_count, cols), f32)
        text_scratch = []
    vmem = pl.BlockSpec(memory_space=pltpu.VMEM)
    smem = pl.BlockSpec(memory_space=pltpu.SMEM)
    hbm = pl.BlockSpec(memory_space=pltpu.HBM)
    query_grad, key_grad, value_grad, key_text, value_text = pl.pallas_call(
        functools.partial(kernel, tiles, heads, size, fused),
        out_shape=[jax.ShapeDtypeStruct((rows, hidden), bf16)] * 3
        + [text_out] * 2,
        in_specs=[hbm] * 4 + [vmem] + [hbm if fused else vmem] * 2 + [smem] * 2,
        out_specs=[hbm] * 3 + [vmem] * 2,
        scratch_shapes=[
            pltpu.VMEM((3, 2, rows, cols), bf16),
            pltpu.VMEM((3, 2, rows, cols), bf16),
            pltpu.VMEM((2, rows, cols), bf16),
            pltpu.VMEM((2, rows, cols), bf16),
            pltpu.VMEM((3, 2, 16, 2 * rows), f32),
            pltpu.VMEM((3, 16, 2 * rows), f32),
            pltpu.VMEM((2 * rows, cols), f32),
            pltpu.VMEM((2 * rows, cols), f32),
            pltpu.VMEM((3, 2, rows, cols), bf16),
            pltpu.VMEM((2, 2, rows, cols), bf16),
            pltpu.VMEM((3, 2, rows, cols), bf16),
            pltpu.VMEM((2, rows, cols), bf16),
            dma((4,)),
            dma((4,)),
            dma((4,)),
            dma((3, 2)),
            dma((3, 2)),
            dma((2, 2, 2, heads)),
            dma((2, 2, 2, heads)),
            dma((3, 2, heads)),
            dma((3, 2, heads)),
            dma((2, heads)),
            dma((2, heads)),
            pltpu.VMEM((2 * rows, cols), f32),
            pltpu.VMEM((2, rows, cols), bf16),
            dma((4, heads)),
        ]
        + text_scratch,
        compiler_params=pltpu.CompilerParams(
            collective_id=0, has_side_effects=True, vmem_limit_bytes=62 * 1024 * 1024
        ),
        cost_estimate=pl.CostEstimate(
            flops=20 * rows * rows * 7 * hidden, bytes_accessed=16 * rows * hidden, transcendentals=0
        ),
    )(
        queries.reshape(rows, hidden),
        out_grad.reshape(rows, hidden),
        key_rows.reshape(rows, hidden),
        value_rows.reshape(rows, hidden),
        stats,
        text_k,
        text_v,
        text_length,
        window_reach.T,
    )

    grads = tuple(grad.reshape(shape) for grad in (query_grad, key_grad, value_grad))
    if fused:
        return grads + (key_text, value_text)

    def text_total(part):
        whole = jnp.zeros((2, text_count, cols), f32)
        whole = lax.dynamic_update_slice_in_dim(whole, part[None], half, 0)
        whole = whole.transpose(1, 0, 2).reshape(text_count, hidden)
        return lax.psum_scatter(whole, "ta", scatter_dimension=0, tiled=True)

    totals = lax.psum((text_total(key_text), text_total(value_text)), "ha")
    return grads + (totals[0].astype(bf16), totals[1].astype(bf16))


def solution(mesh):
    block = P(("grp", "ta"), "ha", None, None)
    text = P(("grp", "ta"), None)
    return jax.shard_map(
        per_device,
        mesh=mesh,
        in_specs=(block,) * 6 + (text, text, P("grp"), P()),
        out_specs=(block,) * 3 + (text, text),
        check_vma=False,
    )
```

```python
import functools

import jax
import jax.numpy as jnp
from jax import lax
from jax.experimental import pallas as pl
from jax.experimental.pallas import tpu as pltpu
from jax.sharding import PartitionSpec as P

LOG2E = 1.4426950408889634
HIDDEN_LSE = 1e30
MESH_ID = pl.DeviceIdType.MESH
NT = (((1,), (1,)), ((), ()))
NN = (((1,), (0,)), ((), ()))
TN = (((0,), (0,)), ((), ()))


def dot(a, b, dims):
    return lax.dot_general(a, b, dims, preferred_element_type=jnp.float32)


def kernel(
    tiles,
    heads,
    size,
    fused,
    q_in,
    g_in,
    k_in,
    v_in,
    stat_in,
    text_k,
    text_v,
    length,
    reach,
    q_out,
    k_out,
    v_out,
    tk_out,
    tv_out,
    qw,
    gw,
    kw,
    vw,
    sw,
    st,
    ak,
    av,
    dq,
    dk,
    rq,
    rk,
    local_sem,
    pair_send,
    pair_recv,
    stat_send,
    stat_recv,
    far_send,
    far_recv,
    term_send,
    term_recv,
    kv_send,
    kv_recv,
    aq,
    qs,
    out_sem,
    *text_scratch,
):
    rows = q_in.shape[0]
    cols = heads * size
    scaling = size ** (-0.5)
    grp = lax.axis_index("grp")
    t = lax.axis_index("ta")
    ha = lax.axis_index("ha")
    c = lax.rem(ha, 2)
    o = 1 - c
    base = ha - c
    partner = (grp, t, base + o)
    has = (t > 0, t < tiles - 1)
    near = (t - 1, t + 1)

    def group(index):
        return pl.ds(pl.multiple_of(index * cols, 128), cols)

    def head(j):
        return pl.ds(pl.multiple_of(j * size, 128), size)

    def group_head(index, j):
        return pl.ds(pl.multiple_of(index * cols + j * size, 128), size)

    barrier = pltpu.get_barrier_semaphore()
    pl.semaphore_signal(barrier, inc=1, device_id=partner, device_id_type=MESH_ID)
    for d in range(2):

        @pl.when(has[d])
        def _():
            for cc in range(2):
                pl.semaphore_signal(
                    barrier, inc=1, device_id=(grp, near[d], base + cc), device_id_type=MESH_ID
                )

    count = 1 + 2 * jnp.where(t > 0, 1, 0) + 2 * jnp.where(t < tiles - 1, 1, 0)
    if fused:
        (tw, tp, tb, tr, tf, tsb, tz, tfb, to) = text_scratch[:9]
        (tg_send, tg_recv, tx_send, tx_recv, xr_sem, zt_send, zt_recv, fin_send, fin_recv) = (
            text_scratch[9:18]
        )
        tl_sem = text_scratch[18]
        half_rows = tw.shape[3]
        p = lax.div(ha, 2)
        across = (grp, t, lax.rem(ha + 2, 4))
        diagonal = (grp, t, 2 * (1 - p) + o)
        for place in (across, diagonal):
            pl.semaphore_signal(barrier, inc=1, device_id=place, device_id_type=MESH_ID)
        for tt in range(tiles):

            @pl.when((t - tt) * (t - tt) > 1)
            def _():
                pl.semaphore_signal(
                    barrier, inc=1, device_id=(grp, tt, ha), device_id_type=MESH_ID
                )

        count = tiles + 2 + jnp.where(t > 0, 1, 0) + jnp.where(t < tiles - 1, 1, 0)
    pl.semaphore_wait(barrier, count)

    def elsewhere(action):
        for tt in range(tiles):

            @pl.when(t != tt)
            def _():
                action(tt)

    if fused:

        def text_gather(a, tt):
            return pltpu.make_async_remote_copy(
                src_ref=(text_k, text_v)[a].at[
                    pl.ds(pl.multiple_of(p * half_rows, half_rows), half_rows), group(c)
                ],
                dst_ref=tw.at[t, p, a],
                send_sem=tg_send.at[a, tt],
                recv_sem=tg_recv.at[a, t],
                device_id=(grp, tt, ha),
                device_id_type=MESH_ID,
            )

        def text_own(a, hh):
            return pltpu.make_async_copy(
                (text_k, text_v)[a].at[pl.ds(hh * half_rows, half_rows), group(c)],
                tw.at[t, hh, a],
                tl_sem.at[a, hh],
            )

        def text_across(tt):
            return pltpu.make_async_remote_copy(
                src_ref=tw.at[tt, p],
                dst_ref=tw.at[tt, p],
                send_sem=tx_send.at[tt],
                recv_sem=tx_recv.at[tt],
                device_id=across,
                device_id_type=MESH_ID,
            )

        sum_across = pltpu.make_async_remote_copy(
            src_ref=tb.at[1 - p],
            dst_ref=tr,
            send_sem=xr_sem.at[0],
            recv_sem=xr_sem.at[1],
            device_id=across,
            device_id_type=MESH_ID,
        )

        def sum_along(tt):
            return pltpu.make_async_remote_copy(
                src_ref=tsb.at[tt],
                dst_ref=tz.at[t],
                send_sem=zt_send.at[tt],
                recv_sem=zt_recv.at[t],
                device_id=(grp, tt, ha),
                device_id_type=MESH_ID,
            )

        def spread(k):
            return pltpu.make_async_remote_copy(
                src_ref=tfb,
                dst_ref=to.at[c, p],
                send_sem=fin_send.at[k],
                recv_sem=fin_recv.at[c, p],
                device_id=(partner, across, diagonal)[k],
                device_id_type=MESH_ID,
            )

        def arrival(ref, sem):
            pltpu.make_async_copy(ref, ref, sem).wait()

    def far(d, cc, a, j):
        src = (q_in, g_in)[a]
        dst = (qw, gw)[a]
        return pltpu.make_async_remote_copy(
            src_ref=src.at[:, group_head(cc, j)],
            dst_ref=dst.at[2 - d, c, :, head(j)],
            send_sem=far_send.at[d, cc, a, j],
            recv_sem=far_recv.at[1 - d, c, a, j],
            device_id=(grp, near[d], base + cc),
            device_id_type=MESH_ID,
        )

    def far_wait(d, b, a, j):
        dst = (qw, gw)[a].at[1 + d, b, :, head(j)]
        pltpu.make_async_copy(dst, dst, far_recv.at[d, b, a, j]).wait()

    def stat_far(d, cc):
        return pltpu.make_async_remote_copy(
            src_ref=stat_in.at[cc],
            dst_ref=sw.at[2 - d, c],
            send_sem=stat_send.at[1 + d, cc],
            recv_sem=stat_recv.at[2 - d, c],
            device_id=(grp, near[d], base + cc),
            device_id_type=MESH_ID,
        )

    def pair(a):
        src = (q_in, g_in, k_in, v_in)[a]
        dst = (qw.at[0, c], gw.at[0, c], kw.at[c], vw.at[c])[a]
        return pltpu.make_async_remote_copy(
            src_ref=src.at[:, group(o)],
            dst_ref=dst,
            send_sem=pair_send.at[a],
            recv_sem=pair_recv.at[a],
            device_id=partner,
            device_id_type=MESH_ID,
        )

    def own(a):
        src = (q_in, g_in, k_in, v_in)[a]
        dst = (qw.at[0, c], gw.at[0, c], kw.at[c], vw.at[c])[a]
        return pltpu.make_async_copy(src.at[:, group(c)], dst, local_sem.at[a])

    stat_pair = pltpu.make_async_remote_copy(
        src_ref=stat_in.at[o],
        dst_ref=sw.at[0, c],
        send_sem=stat_send.at[0, 0],
        recv_sem=stat_recv.at[0, 0],
        device_id=partner,
        device_id_type=MESH_ID,
    )

    stat_pair.start()
    if fused:

        def send_text(tt):
            for a in range(2):
                text_gather(a, tt).start()

        elsewhere(send_text)
        for a in range(2):
            for hh in range(2):
                text_own(a, hh).start()
    for a in range(4):
        pair(a).start()
        own(a).start()
    for d in range(2):

        @pl.when(has[d])
        def _():
            for cc in range(2):
                stat_far(d, cc).start()

    def send_far(j, carry):
        for d in range(2):

            @pl.when(has[d])
            def _():
                for a in range(2):
                    for cc in range(2):
                        far(d, cc, a, j).start()

        return carry

    lax.fori_loop(0, heads, send_far, 0)

    for d in range(2):

        @pl.when(jnp.logical_not(has[d]))
        def _():
            rq[1 + d] = jnp.zeros_like(rq[1 + d])

    if fused:
        def forward_text(tt):
            for a in range(2):
                arrival(tw.at[tt, p, a], tg_recv.at[a, tt])
            text_across(tt).start()

        elsewhere(forward_text)

    for a in range(4):
        own(a).wait()
        pair(a).wait_recv()
    stat_pair.wait_recv()
    def fill(s, values):
        st[s, 0:8] = values[0:8] * LOG2E
        st[s, 8:16] = values[8:16]

    fill(0, stat_in[c] + sw[0, o])

    def term(s, b, j):
        target = partner if s == 0 else (grp, near[s - 1], base + b)
        slot = (0, 2, 1)[s]
        return pltpu.make_async_remote_copy(
            src_ref=dq.at[s, b, :, head(j)],
            dst_ref=rq.at[slot, c, :, head(j)],
            send_sem=term_send.at[s, 0 if s == 0 else b, j],
            recv_sem=term_recv.at[slot, c, j],
            device_id=target,
            device_id_type=MESH_ID,
        )

    def term_wait(slot, group_index, j):
        dst = rq.at[slot, group_index, :, head(j)]
        pltpu.make_async_copy(dst, dst, term_recv.at[slot, group_index, j]).wait()

    def kv(a, j):
        return pltpu.make_async_remote_copy(
            src_ref=dk.at[a, o, :, head(j)],
            dst_ref=rk.at[a, :, head(j)],
            send_sem=kv_send.at[a, j],
            recv_sem=kv_recv.at[a, j],
            device_id=partner,
            device_id_type=MESH_ID,
        )

    def both(ref, j):
        return ref[:, :, head(j)].reshape(2 * rows, size)

    def grads(q, g, k, v, lse, out_dot, ok):
        weight = jnp.exp2(dot(k, q, NT) * (scaling * LOG2E) - lse)
        if ok is not None:
            weight = jnp.where(ok, weight, 0.0)
        score = (weight * (dot(v, g, NT) - out_dot) * scaling).astype(jnp.bfloat16)
        prob = weight.astype(jnp.bfloat16)
        return dot(score, k, TN), dot(score, q, NN), dot(prob, g, NN)

    text_count = tiles * text_k.shape[0] if fused else text_k.shape[0]
    text_ok = lax.broadcasted_iota(jnp.int32, (text_count, 1), 0) < length[0]

    def stats(s, j):
        return st[s, pl.ds(j, 1), :], st[s, pl.ds(8 + j, 1), :]

    def near_step(j, carry):
        q, g = both(qw.at[0], j), both(gw.at[0], j)
        lse, out_dot = stats(0, j)
        dq_own, dk_own, dv_own = grads(q, g, both(kw, j), both(vw, j), lse, out_dot, None)
        ak[:, head(j)] = dk_own
        av[:, head(j)] = dv_own
        aq[:, head(j)] = dq_own
        return carry

    def text_step(j, carry):
        q, g = both(qw.at[0], j), both(gw.at[0], j)
        lse, out_dot = stats(0, j)
        if fused:
            tk = tw[:, :, 0, :, head(j)].reshape(text_count, size)
            tv = tw[:, :, 1, :, head(j)].reshape(text_count, size)
        else:
            tk, tv = text_k[:, group_head(c, j)], text_v[:, group_head(c, j)]
        dq_text, dk_text, dv_text = grads(q, g, tk, tv, lse, out_dot, text_ok)
        if fused:
            for a, part in enumerate((dk_text, dv_text)):
                for tt in range(tiles):
                    for hh in range(2):
                        low = (2 * tt + hh) * half_rows
                        piece = part[low : low + half_rows]
                        tp[hh, tt, a, :, head(j)] = piece
                        tb[hh, tt, a, :, head(j)] = piece.astype(jnp.bfloat16)
        else:
            tk_out[:, head(j)] = dk_text
            tv_out[:, head(j)] = dv_text
        total = (aq[:, head(j)] + dq_text).astype(jnp.bfloat16)
        dq[0, :, :, head(j)] = total.reshape(2, rows, size)
        term(0, o, j).start()
        return carry

    lax.fori_loop(0, heads, near_step, 0)
    if fused:
        elsewhere(lambda tt: arrival(tw.at[tt, 1 - p], tx_recv.at[tt]))
        for a in range(2):
            for hh in range(2):
                text_own(a, hh).wait()
    lax.fori_loop(0, heads, text_step, 0)
    if fused:
        sum_across.start()

    for d in range(2):

        @pl.when(has[d])
        def _():
            for b in range(2):
                dst = sw.at[1 + d, b]
                pltpu.make_async_copy(dst, dst, stat_recv.at[1 + d, b]).wait()
            fill(1 + d, sw[1 + d, 0] + sw[1 + d, 1])

    def far_step(j, carry):
        for d in range(2):

            @pl.when(has[d])
            def _():
                for a in range(2):
                    for b in range(2):
                        far_wait(d, b, a, j)
                seen = reach[1 - d, c * heads + j] >= 1
                lse = st[1 + d, pl.ds(j, 1), :] + jnp.where(seen, 0.0, HIDDEN_LSE)
                out_dot = st[1 + d, pl.ds(8 + j, 1), :]
                dq_far, dk_far, dv_far = grads(
                    both(qw.at[1 + d], j),
                    both(gw.at[1 + d], j),
                    both(kw, j),
                    both(vw, j),
                    lse,
                    out_dot,
                    None,
                )
                ak[:, head(j)] += dk_far
                av[:, head(j)] += dv_far
                dq[1 + d, :, :, head(j)] = (
                    dq_far.astype(jnp.bfloat16).reshape(2, rows, size)
                )
                for b in range(2):
                    term(1 + d, b, j).start()

        dk[0, :, :, head(j)] = (
            ak[:, head(j)].astype(jnp.bfloat16).reshape(2, rows, size)
        )
        dk[1, :, :, head(j)] = av[:, head(j)].astype(jnp.bfloat16).reshape(2, rows, size)
        for a in range(2):
            kv(a, j).start()
        return carry

    early = 2
    lax.fori_loop(0, early, far_step, 0)
    if fused:
        sum_across.wait_recv()
        for tt in range(tiles):
            tsb[tt] = (tp[p, tt] + tr[tt].astype(jnp.float32)).astype(jnp.bfloat16)
        tf[...] = tp[p, t] + tr[t].astype(jnp.float32)
        elsewhere(lambda tt: sum_along(tt).start())
    lax.fori_loop(early, heads, far_step, 0)
    if fused:

        def add_sum(tt):
            arrival(tz.at[tt], zt_recv.at[tt])
            tf[...] += tz[tt].astype(jnp.float32)

        elsewhere(add_sum)
        tfb[...] = tf[...].astype(jnp.bfloat16)
        for k in range(3):
            spread(k).start()
        to[c, p] = tfb[...]

    def put(a, index, source):
        return pltpu.make_async_copy(
            source, (k_out, v_out)[a].at[:, group(index)], out_sem.at[a, index]
        )

    for a in range(2):
        put(a, c, dk.at[a, c]).start()

    def finish_kv(j, carry):
        for a in range(2):
            kv(a, j).wait()
        return carry

    lax.fori_loop(0, heads, finish_kv, 0)
    for a in range(2):
        put(a, o, rk.at[a]).start()
    stat_pair.wait_send()
    for a in range(4):
        pair(a).wait_send()
    for d in range(2):

        @pl.when(has[d])
        def _():
            for cc in range(2):
                stat_far(d, cc).wait_send()

    if fused:
        for cc, pp in ((o, p), (c, 1 - p), (o, 1 - p)):
            arrival(to.at[cc, pp], fin_recv.at[cc, pp])
        for hh in range(2):
            for cc in range(2):
                spot = pl.ds(hh * half_rows, half_rows), pl.ds(cc * cols, cols)
                tk_out[spot] = to[cc, hh, 0]
                tv_out[spot] = to[cc, hh, 1]
        for k in range(3):
            spread(k).wait_send()
        sum_across.wait_send()

        def end_text(tt):
            for a in range(2):
                text_gather(a, tt).wait_send()
            text_across(tt).wait_send()
            sum_along(tt).wait_send()

        elsewhere(end_text)

    def total(own_part, index, j):
        return (
            own_part.astype(jnp.float32)
            + rq[1, index, :, head(j)].astype(jnp.float32)
            + rq[2, index, :, head(j)].astype(jnp.float32)
        ).astype(jnp.bfloat16)

    def put_query(index, j):
        return pltpu.make_async_copy(
            qs.at[index, :, head(j)],
            q_out.at[:, group_head(index, j)],
            out_sem.at[2 + index, j],
        )

    def finish(j, carry):
        term(0, o, j).wait_send()
        term_wait(0, o, j)
        for d in range(2):

            @pl.when(has[d])
            def _():
                for b in range(2):
                    for a in range(2):
                        far(d, b, a, j).wait_send()
                    term_wait(1 + d, b, j)

        qs[c, :, head(j)] = total(dq[0, c, :, head(j)], c, j)
        qs[o, :, head(j)] = total(rq[0, o, :, head(j)], o, j)
        for index in range(2):
            put_query(index, j).start()
        return carry

    lax.fori_loop(0, heads, finish, 0)

    def finish_send(j, carry):
        for d in range(2):

            @pl.when(has[d])
            def _():
                for b in range(2):
                    term(1 + d, b, j).wait_send()

        for index in range(2):
            put_query(index, j).wait()
        return carry

    lax.fori_loop(0, heads, finish_send, 0)
    for a in range(2):
        put(a, c, dk.at[a, c]).wait()
        put(a, o, rk.at[a]).wait()


def per_device(
    queries,
    key_rows,
    value_rows,
    out_grad,
    logsumexp,
    out_dot,
    text_keys,
    text_values,
    text_length,
    window_reach,
):
    shape = queries.shape
    hidden = shape[3]
    rows = shape[0] * shape[1] * shape[2]
    head_count = logsumexp.shape[3]
    size = hidden // head_count
    heads = head_count // 2
    cols = heads * size
    tiles = lax.axis_size("ta")
    half = lax.axis_index("ha") % 2

    def stat(values):
        turned = values.reshape(rows, head_count).T.reshape(2, heads, rows)
        return jnp.pad(turned, ((0, 0), (0, 8 - heads), (0, 0)))

    stats = jnp.concatenate([stat(logsumexp), stat(out_dot)], axis=1)
    empty = jnp.zeros_like(stats)
    stats = jnp.where(
        half == 0,
        jnp.concatenate([stats, empty], axis=2),
        jnp.concatenate([empty, stats], axis=2),
    )
    text_rows = text_keys.shape[0]
    text_count = tiles * text_rows
    half_rows = text_rows // 2
    fused = lax.axis_size("ha") == 4 and text_rows % 32 == 0
    bf16, f32 = jnp.bfloat16, jnp.float32
    dma = pltpu.SemaphoreType.DMA
    if fused:
        text_k, text_v = text_keys, text_values
        text_out = jax.ShapeDtypeStruct((text_rows, hidden), bf16)
        text_scratch = [
            pltpu.VMEM((tiles, 2, 2, half_rows, cols), bf16),
            pltpu.VMEM((2, tiles, 2, half_rows, cols), f32),
            pltpu.VMEM((2, tiles, 2, half_rows, cols), bf16),
            pltpu.VMEM((tiles, 2, half_rows, cols), bf16),
            pltpu.VMEM((2, half_rows, cols), f32),
            pltpu.VMEM((tiles, 2, half_rows, cols), bf16),
            pltpu.VMEM((tiles, 2, half_rows, cols), bf16),
            pltpu.VMEM((2, half_rows, cols), bf16),
            pltpu.VMEM((2, 2, 2, half_rows, cols), bf16),
            dma((2, tiles)),
            dma((2, tiles)),
            dma((tiles,)),
            dma((tiles,)),
            dma((2,)),
            dma((tiles,)),
            dma((tiles,)),
            dma((3,)),
            dma((2, 2)),
            dma((2, 2)),
        ]
    else:
        text_k = lax.all_gather(text_keys, "ta", axis=0, tiled=True)
        text_v = lax.all_gather(text_values, "ta", axis=0, tiled=True)
        text_out = jax.ShapeDtypeStruct((text_count, cols), f32)
        text_scratch = []
    vmem = pl.BlockSpec(memory_space=pltpu.VMEM)
    smem = pl.BlockSpec(memory_space=pltpu.SMEM)
    hbm = pl.BlockSpec(memory_space=pltpu.HBM)
    query_grad, key_grad, value_grad, key_text, value_text = pl.pallas_call(
        functools.partial(kernel, tiles, heads, size, fused),
        out_shape=[jax.ShapeDtypeStruct((rows, hidden), bf16)] * 3
        + [text_out] * 2,
        in_specs=[hbm] * 4 + [vmem] + [hbm if fused else vmem] * 2 + [smem] * 2,
        out_specs=[vmem] * 5,
        scratch_shapes=[
            pltpu.VMEM((3, 2, rows, cols), bf16),
            pltpu.VMEM((3, 2, rows, cols), bf16),
            pltpu.VMEM((2, rows, cols), bf16),
            pltpu.VMEM((2, rows, cols), bf16),
            pltpu.VMEM((3, 2, 16, 2 * rows), f32),
            pltpu.VMEM((3, 16, 2 * rows), f32),
            pltpu.VMEM((2 * rows, cols), f32),
            pltpu.VMEM((2 * rows, cols), f32),
            pltpu.VMEM((3, 2, rows, cols), bf16),
            pltpu.VMEM((2, 2, rows, cols), bf16),
            pltpu.VMEM((3, 2, rows, cols), bf16),
            pltpu.VMEM((2, rows, cols), bf16),
            dma((4,)),
            dma((4,)),
            dma((4,)),
            dma((3, 2)),
            dma((3, 2)),
            dma((2, 2, 2, heads)),
            dma((2, 2, 2, heads)),
            dma((3, 2, heads)),
            dma((3, 2, heads)),
            dma((2, heads)),
            dma((2, heads)),
            pltpu.VMEM((2 * rows, cols), f32),
            pltpu.VMEM((2, rows, cols), bf16),
            dma((4, heads)),
        ]
        + text_scratch,
        compiler_params=pltpu.CompilerParams(
            collective_id=0, has_side_effects=True, vmem_limit_bytes=412 * 128 * 1024
        ),
        cost_estimate=pl.CostEstimate(
            flops=20 * rows * rows * 7 * hidden, bytes_accessed=16 * rows * hidden, transcendentals=0
        ),
    )(
        queries.reshape(rows, hidden),
        out_grad.reshape(rows, hidden),
        key_rows.reshape(rows, hidden),
        value_rows.reshape(rows, hidden),
        stats,
        text_k,
        text_v,
        text_length,
        window_reach.T,
    )

    grads = tuple(grad.reshape(shape) for grad in (query_grad, key_grad, value_grad))
    if fused:
        return grads + (key_text, value_text)

    def text_total(part):
        whole = jnp.zeros((2, text_count, cols), f32)
        whole = lax.dynamic_update_slice_in_dim(whole, part[None], half, 0)
        whole = whole.transpose(1, 0, 2).reshape(text_count, hidden)
        return lax.psum_scatter(whole, "ta", scatter_dimension=0, tiled=True)

    totals = lax.psum((text_total(key_text), text_total(value_text)), "ha")
    return grads + (totals[0].astype(bf16), totals[1].astype(bf16))


def solution(mesh):
    block = P(("grp", "ta"), "ha", None, None)
    text = P(("grp", "ta"), None)
    return jax.shard_map(
        per_device,
        mesh=mesh,
        in_specs=(block,) * 6 + (text, text, P("grp"), P()),
        out_specs=(block,) * 3 + (text, text),
        check_vma=False,
    )
```
